256 devices in a mesh: row: 8 (over x, core), col: 8 (over z), depth: 4 (over y).
Axes of the slice: x: 4, y: 4, z: 8, core: 2. Of those that a mesh axis runs over, the one named last changes fastest.
Arguments:
- inputs: bfloat16 [4, 1024, 8192], P('depth', 'row', 'col'), may hold values from -120 to 120
- w_query: bfloat16 [8192, 8192], P(('row', 'depth'), 'col'), may hold values from -2 to 2
- w_key: bfloat16 [8192, 1024], P(('row', 'depth'), 'col'), may hold values from -1 to 1
- w_value: bfloat16 [8192, 1024], P(('row', 'depth'), 'col'), may hold values from -0.0625 to 0.0625
- upstream: bfloat16 [4, 1024, 8192], P('depth', 'row', 'col'), may hold values from -6 to 6
- sources: int32 [4, 1024], P('depth', 'row'), may hold values from 0 to 15
- tilt: float32 [16], replicated, may hold values from 0.25 to 4
Outputs:
- context: bfloat16 [4, 1024, 8192], P('depth', 'row', 'col')
- grad_query: bfloat16 [8192, 8192], P(('row', 'depth'), 'col')
- grad_key: bfloat16 [8192, 1024], P(('row', 'depth'), 'col')
- grad_value: bfloat16 [8192, 1024], P(('row', 'depth'), 'col')
The draws below stay inside these ranges and needn't reach their ends.
All inputs are finite; a program needn't handle non-finite values.
Results may differ from the reference program's by a relative error of at most 0.025.
The reference program's roundings to bfloat16 on the way count: a program that leaves them out, or rounds other values in their place, can miss the bound.
Values may be sent and summed in bfloat16 or wider, within the bound.
No kernel may reach another device: no remote copies, remote signals or barrier semaphores. Data moves between devices by JAX's collectives and lax.ppermute only.
A program may use at most 128 MiB of HBM per device.

```python
import math
import jax
import jax.numpy as jnp
from jax import lax

D = 8192
H = 64
KVH = 8
HD = 128
SOURCES = 16
LEN = 1024
SEQS = 4


def shared_key_weight(key):
    raw = jnp.clip(jax.random.normal(key, (D, KVH * HD), jnp.float32), -5.0, 5.0) * D ** (-0.5)
    return jnp.clip(raw, -1.0, 1.0)


def draw_inputs(key, part):
    key = jax.random.fold_in(key, 5)
    base_key, scale_key = jax.random.split(key, 2)
    feature_ramp = 3.0 ** (jnp.arange(D, dtype=jnp.float32) / (D - 1))
    base_values = jnp.clip(jax.random.normal(base_key, (SEQS, LEN, D), jnp.float32), -4.0, 4.0)
    row_scale = 10.0 ** jax.random.uniform(scale_key, (SEQS, LEN, 1), jnp.float32)
    return (base_values * feature_ramp * row_scale).astype(jnp.bfloat16)


def draw_w_key(key, part):
    shared = shared_key_weight(key)
    return shared.astype(jnp.bfloat16)


def draw_w_query(key, part):
    key = jax.random.fold_in(key, 7)
    noise_key = jax.random.fold_in(key, 0)
    noise_part = jnp.clip(jax.random.normal(noise_key, (D, H * HD), jnp.float32), -5.0, 5.0) * D ** (-0.5)
    return jnp.clip(noise_part, -2.0, 2.0).astype(jnp.bfloat16)


def plant(entries, rng, low, largest):
    place = [jax.random.randint(jax.random.fold_in(rng, axis), (), 0, length) for axis, length in enumerate(entries.shape)]
    longest = entries.shape.index(max(entries.shape))
    beside = place[:longest] + [(place[longest] + 1) % entries.shape[longest]] + place[longest + 1:]
    return entries.at[tuple(place)].set(low).at[tuple(beside)].set(largest)


def block_levels(rng, dims, cuts, smallest, largest):
    level = 1.0
    for position, blocks in cuts:
        steps = jax.random.uniform(jax.random.fold_in(jax.random.fold_in(rng, 6), position), (blocks,), jnp.float32, smallest / len(cuts), largest / len(cuts))
        level = level * jnp.repeat(jnp.exp(steps), dims[position] // blocks).reshape((-1,) + (1,) * (len(dims) - 1 - position))
    return level


def normal_values(rng, dims, width, most, cuts=(), kind=jnp.bfloat16):
    result = width * jax.random.normal(rng, dims, jnp.float32)
    if cuts:
        result = result * block_levels(rng, dims, cuts, -0.22, 0.18)
    return jnp.clip(result, -most, most).astype(kind)


def setup_inputs(seed: int = 0) -> dict:
    streams_of = jax.random.split(jax.random.key(seed), 8)
    inputs = draw_inputs(jax.random.fold_in(streams_of[7], 71), 0)
    w_query = draw_w_query(jax.random.fold_in(streams_of[7], 71), 0)
    w_key = draw_w_key(jax.random.fold_in(streams_of[7], 71), 0)
    w_value = normal_values(streams_of[3], (D, KVH * HD), D ** -0.5, 0.0625, ((0, 32), (1, 8)))
    upstream = normal_values(streams_of[4], (SEQS, LEN, H * HD), 1.0, 6.0, ((0, 4), (1, 8), (2, 8)))
    sources = plant(jax.random.randint(streams_of[5], (SEQS, LEN), 0, SOURCES), jax.random.fold_in(streams_of[5], 1), 0, SOURCES - 1).astype(jnp.int32)
    tilt = jnp.clip(jnp.exp(jax.random.uniform(streams_of[6], (SOURCES,), jnp.float32, math.log(0.25), math.log(4.0))), 0.25, 4.0)
    return dict(inputs=inputs, w_query=w_query, w_key=w_key, w_value=w_value, upstream=upstream, sources=sources, tilt=tilt)


norm_epsilon = 1e-05
rope_base = 10000.0

def rotate(value_rows, positions, direction):
    count_rows = value_rows.shape[0]
    head_count = value_rows.shape[1] // HD
    half_width = HD // 2
    frequency = rope_base ** (-jnp.arange(half_width, dtype=jnp.float32) * 2.0 / HD)
    angles = positions.astype(jnp.float32)[:, None] * frequency[None, :]
    cosine = jnp.cos(angles)[:, None, :]
    sine_part = direction * jnp.sin(angles)[:, None, :]
    shaped = value_rows.reshape(count_rows, head_count, HD)
    first_half = shaped[..., :half_width]
    second_half = shaped[..., half_width:]
    rotated = jnp.concatenate([first_half * cosine - second_half * sine_part, second_half * cosine + first_half * sine_part], axis=-1)
    return rotated.reshape(count_rows, head_count * HD)

def settle(partial_sum):
    return lax.optimization_barrier(partial_sum.astype(jnp.bfloat16)).astype(jnp.float32)

def head_pass(packed):
    query_block, key_block, value_block, cotangent_block = packed
    query_wide = query_block.astype(jnp.float32)
    key_wide = key_block.astype(jnp.float32)
    value_wide = value_block.astype(jnp.float32)
    cotangent_wide = cotangent_block.astype(jnp.float32)
    length = query_block.shape[0]
    scores = jnp.einsum('trd,sd->rts', query_wide, key_wide) / math.sqrt(HD)
    causal = jnp.arange(length)[None, :] <= jnp.arange(length)[:, None]
    scores = jnp.where(causal[None], scores, -jnp.inf)
    row_max = lax.optimization_barrier(jnp.max(scores, axis=-1, keepdims=True))
    exponent = jnp.exp(scores - row_max)
    attention = exponent / lax.optimization_barrier(jnp.sum(exponent, axis=-1, keepdims=True))
    attention_portion = lax.optimization_barrier(attention.astype(jnp.bfloat16)).astype(jnp.float32)
    context = jnp.einsum('rts,sd->trd', attention_portion, value_wide)
    dprobs = jnp.einsum('trd,sd->rts', cotangent_wide, value_wide)
    row_delta = lax.optimization_barrier(jnp.sum(dprobs * attention, axis=-1, keepdims=True))
    score_gradient = attention * (dprobs - row_delta) / math.sqrt(HD)
    score_gradient = lax.optimization_barrier(score_gradient.astype(jnp.bfloat16)).astype(jnp.float32)
    value_grad = jnp.einsum('rts,trd->sd', attention_portion, cotangent_wide)
    key_grad = jnp.einsum('rts,trd->sd', score_gradient, query_wide)
    query_grad = jnp.einsum('rts,sd->trd', score_gradient, key_wide)
    return (context, query_grad, key_grad, value_grad)

def reference(inputs, w_query, w_key, w_value, upstream, sources, tilt):
    group_size = H // KVH
    positions = jnp.arange(LEN, dtype=jnp.int32)
    total_query = jnp.zeros((D, H * HD), jnp.float32)
    total_key = jnp.zeros((D, KVH * HD), jnp.float32)
    total_value = jnp.zeros((D, KVH * HD), jnp.float32)
    contexts = []
    for sequence in range(SEQS):
        as_float = inputs[sequence].astype(jnp.float32)
        normed = (as_float * lax.rsqrt(lax.optimization_barrier(jnp.mean(as_float * as_float, axis=1, keepdims=True)) + norm_epsilon)).astype(jnp.bfloat16)
        query = rotate(jnp.dot(normed, w_query, preferred_element_type=jnp.float32), positions, 1.0).astype(jnp.bfloat16)
        keys = rotate(jnp.dot(normed, w_key, preferred_element_type=jnp.float32), positions, 1.0).astype(jnp.bfloat16)
        value_rows = jnp.dot(normed, w_value, preferred_element_type=jnp.float32).astype(jnp.bfloat16)
        source_match = sources[sequence][:, None] == jnp.arange(SOURCES, dtype=jnp.int32)[None, :]
        token_weight = lax.optimization_barrier(jnp.sum(jnp.where(source_match, tilt[None, :], 0.0), axis=1))
        cotangent = (upstream[sequence].astype(jnp.float32) * token_weight[:, None]).astype(jnp.bfloat16)
        query_per_head = query.reshape(LEN, KVH, group_size, HD).transpose(1, 0, 2, 3)
        key_per_head = keys.reshape(LEN, KVH, HD).transpose(1, 0, 2)
        value_per_head = value_rows.reshape(LEN, KVH, HD).transpose(1, 0, 2)
        cotangent_per_head = cotangent.reshape(LEN, KVH, group_size, HD).transpose(1, 0, 2, 3)
        context, query_grad, key_grad, value_grad = lax.map(head_pass, (query_per_head, key_per_head, value_per_head, cotangent_per_head))
        contexts.append(context.transpose(1, 0, 2, 3).reshape(LEN, H * HD).astype(jnp.bfloat16))
        query_grad = rotate(query_grad.transpose(1, 0, 2, 3).reshape(LEN, H * HD), positions, -1.0).astype(jnp.bfloat16)
        key_grad = rotate(key_grad.transpose(1, 0, 2).reshape(LEN, KVH * HD), positions, -1.0).astype(jnp.bfloat16)
        value_grad = value_grad.transpose(1, 0, 2).reshape(LEN, KVH * HD).astype(jnp.bfloat16)
        total_query = total_query + settle(jnp.dot(normed.T, query_grad, preferred_element_type=jnp.float32))
        total_key = total_key + settle(jnp.dot(normed.T, key_grad, preferred_element_type=jnp.float32))
        total_value = total_value + settle(jnp.dot(normed.T, value_grad, preferred_element_type=jnp.float32))
    return (jnp.stack(contexts), total_query.astype(jnp.bfloat16), total_key.astype(jnp.bfloat16), total_value.astype(jnp.bfloat16))
```

```python
import functools
import math

import jax
import jax.numpy as jnp
from jax import lax
from jax.experimental import pallas as pl
from jax.experimental.pallas import tpu as pltpu
from jax.sharding import PartitionSpec as P

D = 8192
HD = 128
ROWS = 8
COLS = 8
DEPTHS = 4
CHIPS = 4

norm_epsilon = 1e-05
rope_base = 10000.0

SKEW = (0, 1, 7, 2, 6, 3, 5, 4)
SLOT_ROW = tuple(SKEW.index(k) for k in range(8))

BF = jnp.bfloat16
F32 = jnp.float32
VMEM = pl.BlockSpec(memory_space=pltpu.VMEM)
SMEM = pl.BlockSpec(memory_space=pltpu.SMEM)
PARAMS = pltpu.CompilerParams(vmem_limit_bytes=48 * 1024 * 1024)


def shift(value, axis, step, size):
    return lax.ppermute(value, axis, [(i, (i + step) % size) for i in range(size)])


def to_chip(value, step):
    return shift(value, "row", 2 * step, ROWS)


def to_sibling(value):
    return lax.ppermute(value, "row", [(i, i ^ 1) for i in range(ROWS)])


def transpose_blocks(value):
    pairs = [
        (r * COLS + c, c * COLS + (c + SKEW[r]) % COLS) for r in range(ROWS) for c in range(COLS)
    ]
    return lax.ppermute(value, ("row", "col"), pairs)


def gather_row(value):
    pair = jnp.concatenate([value, to_sibling(value)], axis=0)
    pairs = [pair] + [to_chip(pair, -step) for step in range(1, CHIPS)]
    count = value.shape[0]
    return jnp.concatenate([p[:count] for p in pairs] + [p[count:] for p in pairs], axis=0)


def scatter_chips(blocks):
    parts = [blocks[0]] + [to_chip(blocks[step], step) for step in range(1, CHIPS)]
    return parts


def assemble_kernel(meta, scale, *refs):
    blocks, out = refs[:8], refs[8]
    count = blocks[0].shape[0]
    for slot in range(8):
        source = pl.multiple_of(meta[slot] * count, count)
        target = pl.multiple_of(meta[8 + slot] * count, count)
        factor = scale[pl.ds(source, count), :]
        for part in range(4):
            lanes = pl.multiple_of(meta[16 + part] * 256, 256)
            value = blocks[slot][:, pl.ds(lanes, 256)].astype(F32)
            for half in range(2):
                at = part * 256 + half * 128
                out[pl.ds(target, count), at : at + 128] = (
                    value[:, half * 128 : half * 128 + 128] * factor
                ).astype(BF)


def assemble(meta, scale, blocks):
    count, width = blocks[0].shape
    return pl.pallas_call(
        assemble_kernel,
        out_shape=jax.ShapeDtypeStruct((8 * count, width), BF),
        in_specs=[SMEM] + [VMEM] * 9,
        out_specs=VMEM,
        compiler_params=PARAMS,
        name="assemble",
    )(meta, scale, *blocks)


def turn(value, cosine, sine):
    return value * cosine + pltpu.roll(value, HD // 2, 1) * sine


def project_kernel(p0, p1, p2, p3, cosine, sine, q_out, kv_out):
    heads = q_out.shape[1] // HD
    c, s = cosine[...], sine[...]
    for h in range(heads + 2):
        lanes = slice(h * HD, (h + 1) * HD)
        total = (p0[:, lanes] + p1[:, lanes]) + (p2[:, lanes] + p3[:, lanes])
        if h < heads:
            q_out[:, lanes] = turn(total, c, s).astype(BF)
        elif h == heads:
            kv_out[:, :HD] = turn(total, c, s).astype(BF)
        else:
            kv_out[:, HD:] = total.astype(BF)


def project(parts, cosine, sine):
    count, width = parts[0].shape
    return pl.pallas_call(
        project_kernel,
        out_shape=(
            jax.ShapeDtypeStruct((count, width - 2 * HD), BF),
            jax.ShapeDtypeStruct((count, 2 * HD), BF),
        ),
        in_specs=[VMEM] * 6,
        out_specs=(VMEM, VMEM),
        compiler_params=PARAMS,
        name="project",
    )(*parts, cosine, sine)


def grad_kernel(p0, p1, p2, p3, cosine, sine, out):
    for h in range(2):
        lanes = slice(h * HD, (h + 1) * HD)
        total = (p0[:, lanes] + p1[:, lanes]) + (p2[:, lanes] + p3[:, lanes])
        if h == 0:
            total = turn(total, cosine[...], -sine[...])
        out[:, lanes] = total.astype(BF)


def finish_grads(parts, cosine, sine):
    return pl.pallas_call(
        grad_kernel,
        out_shape=jax.ShapeDtypeStruct(parts[0].shape, BF),
        in_specs=[VMEM] * 6,
        out_specs=VMEM,
        compiler_params=PARAMS,
        name="finish_grads",
    )(*parts, cosine, sine)


NT = (((1,), (1,)), ((), ()))
NN = (((1,), (0,)), ((), ()))


def mm(a, b, dims=NN):
    return lax.dot_general(a, b, dims, preferred_element_type=F32)


def attention_kernel(
    meta, q_ref, kv_ref, up_ref, weight_ref, cos_ref, sin_ref, ctx_ref, qg_ref, keep_ref, send_ref
):
    count, width = q_ref.shape
    keys = kv_ref.shape[0]
    half = keys // 2
    k = kv_ref[:, :HD]
    v = kv_ref[:, HD:]
    k_t = k.T
    v_t = v.T
    own = meta[8]
    scale = 1.0 / math.sqrt(HD)
    query_at = own * count + lax.broadcasted_iota(jnp.int32, (count, count), 1)
    row_at = lax.broadcasted_iota(jnp.int32, (count, count), 0)
    bias = []
    for block in range(keys // count):
        allowed = meta[block] * count + row_at <= query_at
        bias.append(jnp.where(allowed, 0.0, -jnp.inf))
    bias = jnp.concatenate(bias, axis=0)
    bias = jnp.concatenate([bias, bias], axis=1)
    weight = weight_ref[...]
    dk = dv = None
    for pair in range(width // (2 * HD)):
        first = slice(2 * pair * HD, (2 * pair + 1) * HD)
        second = slice((2 * pair + 1) * HD, (2 * pair + 2) * HD)
        q = jnp.concatenate([q_ref[:, first], q_ref[:, second]], axis=0)
        cot = jnp.concatenate(
            [
                (up_ref[:, first].astype(F32) * weight).astype(BF),
                (up_ref[:, second].astype(F32) * weight).astype(BF),
            ],
            axis=0,
        )
        scores = mm(k, q, NT) * scale + bias
        top = jnp.max(scores, axis=0, keepdims=True)
        exponent = jnp.exp(scores - top)
        attention = exponent * (1.0 / jnp.sum(exponent, axis=0, keepdims=True))
        portion = attention.astype(BF)
        dprobs = mm(v, cot, NT)
        delta = jnp.sum(dprobs * attention, axis=0, keepdims=True)
        dscores = (attention * (dprobs - delta) * scale).astype(BF)
        context = mm(v_t, portion).T
        query_grad = mm(k_t, dscores).T
        ctx_ref[:, first] = context[:count].astype(BF)
        ctx_ref[:, second] = context[count:].astype(BF)
        c, s = cos_ref[...], -sin_ref[...]
        qg_ref[:, first] = turn(query_grad[:count], c, s).astype(BF)
        qg_ref[:, second] = turn(query_grad[count:], c, s).astype(BF)
        dk_part = mm(dscores, q)
        dv_part = mm(portion, cot)
        dk = dk_part if dk is None else dk + dk_part
        dv = dv_part if dv is None else dv + dv_part
    keep_ref[:, :HD] = dk[:half]
    keep_ref[:, HD:] = dv[:half]
    send_ref[:, :HD] = dk[half:]
    send_ref[:, HD:] = dv[half:]


def attend(meta, q, kv, upstream, weight, cosine, sine):
    count, width = q.shape
    half = kv.shape[0] // 2
    return pl.pallas_call(
        attention_kernel,
        out_shape=(
            jax.ShapeDtypeStruct((count, width), BF),
            jax.ShapeDtypeStruct((count, width), BF),
            jax.ShapeDtypeStruct((half, 2 * HD), F32),
            jax.ShapeDtypeStruct((half, 2 * HD), F32),
        ),
        in_specs=[SMEM] + [VMEM] * 6,
        out_specs=(VMEM,) * 4,
        compiler_params=PARAMS,
        name="attention",
    )(meta, q, kv, upstream, weight, cosine, sine)


def shards(inputs, w_query, w_key, w_value, upstream, sources, tilt):
    row = lax.axis_index("row")
    col = lax.axis_index("col")
    depth = lax.axis_index("depth")
    chip, core = row // 2, row % 2
    local = inputs[0]
    count = local.shape[0]
    width = w_query.shape[1]

    block = transpose_blocks(local)
    weights = jnp.concatenate([w_query, w_key, w_value], axis=1)
    weight_parts = [weights] + [shift(weights, "depth", s, DEPTHS) for s in range(1, DEPTHS)]
    wide = local.astype(F32)
    squares = lax.psum(jnp.sum(wide * wide, axis=1)[None], "col")
    slots = {0: block}
    right = left = block
    for step in range(1, 5):
        right = shift(right, "col", 1, COLS)
        slots[step] = right
        if step < 4:
            left = shift(left, "col", -1, COLS)
            slots[8 - step] = left
    squares = lax.all_gather(squares, "row", axis=0, tiled=True).reshape(-1)
    factor = lax.rsqrt(squares / D + norm_epsilon)
    factor = jnp.broadcast_to(factor[:, None], (factor.shape[0], HD))

    slot_ids = (col - jnp.arange(8, dtype=jnp.int32) - row) % 8
    source_rows = jnp.asarray(SLOT_ROW, jnp.int32)[slot_ids]
    places = ((source_rows % 2) ^ core) * 4 + (source_rows // 2 - chip) % 4
    parts = (depth - jnp.arange(4, dtype=jnp.int32)) % 4
    meta = jnp.concatenate([source_rows, places, parts]).astype(jnp.int32)
    features = assemble(meta, factor, [slots[k] for k in range(8)])

    half = features.shape[0] // 2
    whole = jnp.concatenate(weight_parts, axis=0)
    sent = to_sibling(jnp.dot(features[half:], whole, preferred_element_type=F32))
    kept = jnp.dot(features[:half], whole, preferred_element_type=F32)
    blocks = [
        kept[j * count : (j + 1) * count] + sent[j * count : (j + 1) * count] for j in range(CHIPS)
    ]

    positions = (row * count + jnp.arange(count, dtype=jnp.int32)).astype(F32)
    frequency = rope_base ** (-jnp.arange(HD // 2, dtype=F32) * 2.0 / HD)
    angles = positions[:, None] * frequency[None, :]
    cosine = jnp.cos(angles)
    sine = jnp.sin(angles)
    cosine = jnp.concatenate([cosine, cosine], axis=1)
    sine = jnp.concatenate([-sine, sine], axis=1)
    query, kv = project(scatter_chips(blocks), cosine, sine)

    all_kv = gather_row(kv)
    order = jnp.arange(8, dtype=jnp.int32)
    key_rows = 2 * ((chip + order % 4) % 4) + (core ^ (order // 4))
    key_meta = jnp.concatenate([key_rows, row[None]]).astype(jnp.int32)
    match = sources[0][:, None] == jnp.arange(tilt.shape[0], dtype=jnp.int32)[None, :]
    token_weight = jnp.sum(jnp.where(match, tilt[None, :], 0.0), axis=1)
    token_weight = jnp.broadcast_to(token_weight[:, None], (count, HD))
    context, query_grad, keep, send = attend(
        key_meta, query, all_kv, upstream[0], token_weight, cosine, sine
    )

    own = jnp.concatenate(
        [query_grad] + [to_chip(query_grad, -step) for step in range(1, CHIPS)], axis=0
    )
    all_query = jnp.concatenate([own, to_sibling(own)], axis=0)
    other = to_sibling(send)
    kv_blocks = [
        keep[j * count : (j + 1) * count] + other[j * count : (j + 1) * count]
        for j in range(CHIPS)
    ]
    kv_grad = finish_grads(scatter_chips(kv_blocks), cosine, sine)
    all_kv_grad = gather_row(kv_grad)

    def weight_grad(grads):
        term = lax.dot_general(
            features, grads, (((0,), (0,)), ((), ())), preferred_element_type=F32
        ).astype(BF)
        size = term.shape[0] // DEPTHS
        pieces = [term[:size]] + [
            shift(term[s * size : (s + 1) * size], "depth", -s, DEPTHS) for s in range(1, DEPTHS)
        ]
        total = (pieces[0].astype(F32) + pieces[1].astype(F32)) + (
            pieces[2].astype(F32) + pieces[3].astype(F32)
        )
        return total.astype(BF)

    grad_query = weight_grad(all_query)
    grad_pair = weight_grad(all_kv_grad)
    pair = w_key.shape[1]
    return context[None], grad_query, grad_pair[:, :pair], grad_pair[:, pair:]


def solution(mesh):
    in_specs = (
        P("depth", "row", "col"),
        P(("row", "depth"), "col"),
        P(("row", "depth"), "col"),
        P(("row", "depth"), "col"),
        P("depth", "row", "col"),
        P("depth", "row"),
        P(),
    )
    out_specs = (
        P("depth", "row", "col"),
        P(("row", "depth"), "col"),
        P(("row", "depth"), "col"),
        P(("row", "depth"), "col"),
    )
    return jax.shard_map(shards, mesh=mesh, in_specs=in_specs, out_specs=out_specs, check_vma=False)
```

```python
import functools
import math

import jax
import jax.numpy as jnp
from jax import lax
from jax.experimental import pallas as pl
from jax.experimental.pallas import tpu as pltpu
from jax.sharding import PartitionSpec as P

D = 8192
HD = 128
ROWS = 8
COLS = 8
DEPTHS = 4
CHIPS = 4

norm_epsilon = 1e-05
rope_base = 10000.0

SKEW = (0, 1, 7, 2, 6, 3, 5, 4)
SLOT_ROW = tuple(SKEW.index(k) for k in range(8))

BF = jnp.bfloat16
F32 = jnp.float32
VMEM = pl.BlockSpec(memory_space=pltpu.VMEM)
SMEM = pl.BlockSpec(memory_space=pltpu.SMEM)
PARAMS = pltpu.CompilerParams(vmem_limit_bytes=48 * 1024 * 1024)


def shift(value, axis, step, size):
    return lax.ppermute(value, axis, [(i, (i + step) % size) for i in range(size)])


def to_chip(value, step):
    return swap(value, "row", 2 * step)


def to_sibling(value):
    return swap(value, "row", 1)


def swap(value, axis, bit):
    return lax.ppermute(value, axis, [(i, i ^ bit) for i in range(8)])


def place(difference):
    return (difference % 2) * 4 + difference // 2


def transpose_blocks(value):
    pairs = [
        (r * COLS + c, c * COLS + (c + SKEW[r]) % COLS) for r in range(ROWS) for c in range(COLS)
    ]
    return lax.ppermute(value, ("row", "col"), pairs)


def spread(root, rest):
    square = root * root
    return (square * square) * (square * root) * rest


def pack(blocks):
    largest = functools.reduce(
        jnp.maximum, [jnp.max(jnp.abs(b), axis=0, keepdims=True) for b in blocks]
    )
    unit = jnp.maximum(largest, 1e-28) / 16384.0
    root = lax.reduce_precision(unit**0.125, 5, 10)
    rest = lax.reduce_precision(unit / spread(root, jnp.ones_like(root)), 5, 10)
    scale = 1.0 / spread(root, rest)
    tail = jnp.concatenate([root, rest, jnp.zeros((14, root.shape[1]), F32)], axis=0)
    return [jnp.concatenate([b * scale, tail], axis=0).astype(jnp.float16) for b in blocks]


def unpack(message):
    count = message.shape[0] - 16
    wide = message.astype(F32)
    return wide[:count] * spread(wide[count : count + 1], wide[count + 1 : count + 2])


def assemble_kernel(meta, *refs):
    blocks, out = refs[:8], refs[8]
    count = blocks[0].shape[0]
    for slot in range(8):
        target = pl.multiple_of(meta[slot] * count, count)
        for part in range(4):
            lanes = pl.multiple_of(meta[8 + part] * 256, 256)
            out[pl.ds(target, count), part * 256 : part * 256 + 256] = blocks[slot][
                :, pl.ds(lanes, 256)
            ]


def assemble(meta, blocks):
    count, width = blocks[0].shape
    return pl.pallas_call(
        assemble_kernel,
        out_shape=jax.ShapeDtypeStruct((8 * count, width), BF),
        in_specs=[SMEM] + [VMEM] * 8,
        out_specs=VMEM,
        compiler_params=PARAMS,
        name="assemble",
    )(meta, *blocks)


def reorder_kernel(meta, value, out):
    count = value.shape[0] // 8
    for block in range(8):
        target = pl.multiple_of(meta[block] * count, count)
        out[pl.ds(target, count), :] = value[block * count : (block + 1) * count, :]


def reorder(meta, value):
    return pl.pallas_call(
        reorder_kernel,
        out_shape=jax.ShapeDtypeStruct(value.shape, value.dtype),
        in_specs=[SMEM, VMEM],
        out_specs=VMEM,
        compiler_params=PARAMS,
        name="reorder",
    )(meta, value)


def turn(value, cosine, sine):
    return value * cosine + pltpu.roll(value, HD // 2, 1) * sine


def project_kernel(total, cosine, sine, out):
    c, s = cosine[...], sine[...]
    for h in range(out.shape[1] // HD):
        lanes = slice(h * HD, (h + 1) * HD)
        out[:, lanes] = turn(total[:, lanes], c, s).astype(BF)


def pair_kernel(*refs):
    parts, (cosine, sine, out) = refs[:-3], refs[-3:]
    for h in range(2):
        lanes = slice(h * HD, (h + 1) * HD)
        total = functools.reduce(jnp.add, [p[:, lanes] for p in parts])
        if h == 0:
            total = turn(total, cosine[...], sine[...])
        out[:, lanes] = total.astype(BF)


def finish(kernel, name, parts, cosine, sine):
    return pl.pallas_call(
        kernel,
        out_shape=jax.ShapeDtypeStruct(parts[0].shape, BF),
        in_specs=[VMEM] * (len(parts) + 2),
        out_specs=VMEM,
        compiler_params=PARAMS,
        name=name,
    )(*parts, cosine, sine)


def project(total, cosine, sine):
    return finish(project_kernel, "project", [total], cosine, sine)


def project_pair(parts, cosine, sine):
    return finish(pair_kernel, "project_pair", parts, cosine, sine)


NT = (((1,), (1,)), ((), ()))
NN = (((1,), (0,)), ((), ()))


def mm(a, b, dims=NN):
    return lax.dot_general(a, b, dims, preferred_element_type=F32)


def attention_kernel(
    meta, q_ref, kv_ref, up_ref, weight_ref, cos_ref, sin_ref, ctx_ref, qg_ref, keep_ref, send_ref,
    sums_ref,
):
    count, width = q_ref.shape
    keys = kv_ref.shape[0]
    half = keys // 2
    k = kv_ref[:, :HD]
    v = kv_ref[:, HD:]
    k_t = k.T
    v_t = v.T
    own = meta[8]
    scale = 1.0 / math.sqrt(HD)
    query_at = own * count + lax.broadcasted_iota(jnp.int32, (count, count), 1)
    row_at = lax.broadcasted_iota(jnp.int32, (count, count), 0)
    bias = []
    for block in range(keys // count):
        allowed = block * count + row_at <= query_at
        bias.append(jnp.where(allowed, 0.0, -jnp.inf))
    bias = jnp.concatenate(bias, axis=0)
    bias = jnp.concatenate([bias, bias], axis=1)
    weight = weight_ref[...]
    dk = dv = None
    for pair in range(width // (2 * HD)):
        first = slice(2 * pair * HD, (2 * pair + 1) * HD)
        second = slice((2 * pair + 1) * HD, (2 * pair + 2) * HD)
        q = jnp.concatenate([q_ref[:, first], q_ref[:, second]], axis=0)
        cot = jnp.concatenate(
            [
                (up_ref[:, first].astype(F32) * weight).astype(BF),
                (up_ref[:, second].astype(F32) * weight).astype(BF),
            ],
            axis=0,
        )
        scores = mm(k, q, NT) * scale + bias
        top = jnp.max(scores, axis=0, keepdims=True)
        exponent = jnp.exp(scores - top)
        attention = exponent * (1.0 / jnp.sum(exponent, axis=0, keepdims=True))
        portion = attention.astype(BF)
        dprobs = mm(v, cot, NT)
        delta = jnp.sum(dprobs * attention, axis=0, keepdims=True)
        dscores = (attention * (dprobs - delta) * scale).astype(BF)
        context = mm(v_t, portion).T
        query_grad = mm(k_t, dscores).T
        ctx_ref[:, first] = context[:count].astype(BF)
        ctx_ref[:, second] = context[count:].astype(BF)
        c, s = cos_ref[...], -sin_ref[...]
        qg_ref[:, first] = turn(query_grad[:count], c, s).astype(BF)
        qg_ref[:, second] = turn(query_grad[count:], c, s).astype(BF)
        dk_part = mm(dscores, q)
        dv_part = mm(portion, cot)
        dk = dk_part if dk is None else dk + dk_part
        dv = dv_part if dv is None else dv + dv_part
    for block in range(keys // count):
        rows = slice(block * count, (block + 1) * count)
        target = pl.multiple_of(meta[block] * count, count)
        sums_ref[pl.ds(target, count), :HD] = dk[rows]
        sums_ref[pl.ds(target, count), HD:] = dv[rows]
    keep_ref[...] = sums_ref[:half]
    send_ref[...] = sums_ref[half:]


def attend(meta, q, kv, upstream, weight, cosine, sine):
    count, width = q.shape
    half = kv.shape[0] // 2
    return pl.pallas_call(
        attention_kernel,
        out_shape=(
            jax.ShapeDtypeStruct((count, width), BF),
            jax.ShapeDtypeStruct((count, width), BF),
            jax.ShapeDtypeStruct((half, 2 * HD), F32),
            jax.ShapeDtypeStruct((half, 2 * HD), F32),
        ),
        in_specs=[SMEM] + [VMEM] * 6,
        out_specs=(VMEM,) * 4,
        scratch_shapes=[pltpu.VMEM((2 * half, 2 * HD), F32)],
        compiler_params=PARAMS,
        name="attention",
    )(meta, q, kv, upstream, weight, cosine, sine)


def shards(inputs, w_query, w_key, w_value, upstream, sources, tilt):
    row = lax.axis_index("row")
    col = lax.axis_index("col")
    depth = lax.axis_index("depth")
    local = inputs[0]
    count = local.shape[0]
    width = w_query.shape[1]

    wide = local.astype(F32)
    squares = lax.psum(jnp.sum(wide * wide, axis=1)[None], "col")
    normed = (wide * lax.rsqrt(squares / D + norm_epsilon).reshape(-1, 1)).astype(BF)
    block = transpose_blocks(normed)
    weights = jnp.concatenate([w_query, w_key, w_value], axis=1)
    weights = [weights] + [shift(weights, "depth", s, DEPTHS) for s in range(1, DEPTHS)]
    block, weights = lax.optimization_barrier((block, weights))
    slots = {0: block}
    right = left = block
    for step in range(1, 5):
        right = shift(right, "col", 1, COLS)
        slots[step] = right
        if step < 4:
            left = shift(left, "col", -1, COLS)
            slots[8 - step] = left
    weights = jnp.concatenate(weights, axis=0)

    slot_ids = (col - jnp.arange(8, dtype=jnp.int32) - row) % 8
    source_rows = jnp.asarray(SLOT_ROW, jnp.int32)[slot_ids]
    places = place(source_rows ^ row)
    parts = (depth - jnp.arange(4, dtype=jnp.int32)) % 4
    meta = jnp.concatenate([places, parts]).astype(jnp.int32)
    features = assemble(meta, [slots[k] for k in range(8)])

    half = features.shape[0] // 2

    def chip_blocks(kept, sent):
        return [
            kept[j * count : (j + 1) * count] + sent[j * count : (j + 1) * count]
            for j in range(CHIPS)
        ]

    send = jnp.dot(features[half:], weights, preferred_element_type=F32)
    send, features = lax.optimization_barrier((send, features))
    kept = jnp.dot(features[:half], weights, preferred_element_type=F32)
    blocks = chip_blocks(kept, to_sibling(send))
    messages = pack(blocks[1:])
    parts = [unpack(to_chip(messages[j - 1], j)) for j in range(1, CHIPS)]
    total_rows = (blocks[0] + parts[0]) + (parts[1] + parts[2])

    positions = (row * count + jnp.arange(count, dtype=jnp.int32)).astype(F32)
    frequency = rope_base ** (-jnp.arange(HD // 2, dtype=F32) * 2.0 / HD)
    angles = positions[:, None] * frequency[None, :]
    cosine = jnp.cos(angles)
    sine = jnp.sin(angles)
    cosine = jnp.concatenate([cosine, cosine], axis=1)
    sine = jnp.concatenate([-sine, sine], axis=1)
    kv = project_pair([total_rows[:, width:]], cosine, sine)
    all_kv = lax.all_gather(kv, "row", axis=0, tiled=True)
    query = project(total_rows[:, :width], cosine, sine)

    order = jnp.arange(8, dtype=jnp.int32)
    key_places = place(order ^ row)
    key_meta = jnp.concatenate([key_places, row[None]]).astype(jnp.int32)
    match = sources[0][:, None] == jnp.arange(tilt.shape[0], dtype=jnp.int32)[None, :]
    token_weight = jnp.sum(jnp.where(match, tilt[None, :], 0.0), axis=1)
    token_weight = jnp.broadcast_to(token_weight[:, None], (count, HD))
    context, query_grad, keep, send = attend(
        key_meta, query, all_kv, upstream[0], token_weight, cosine, sine
    )

    def term(grads):
        return lax.dot_general(
            features, grads, (((0,), (0,)), ((), ())), preferred_element_type=F32
        ).astype(BF)

    def pieces(whole):
        size = whole.shape[0] // DEPTHS
        return [whole[:size]] + [
            shift(whole[s * size : (s + 1) * size], "depth", -s, DEPTHS) for s in range(1, DEPTHS)
        ]

    def total(parts):
        return (
            (parts[0].astype(F32) + parts[1].astype(F32))
            + (parts[2].astype(F32) + parts[3].astype(F32))
        ).astype(BF)

    own = jnp.concatenate(
        [query_grad] + [to_chip(query_grad, step) for step in range(1, CHIPS)], axis=0
    )
    sums = keep + to_sibling(send)
    near = sums[: 2 * count] + to_chip(sums[2 * count :], 2)
    own, near = lax.optimization_barrier((own, near))
    all_query = jnp.concatenate([own, to_sibling(own)], axis=0)
    next_sum = to_chip(near[count:], 1)
    all_query, next_sum = lax.optimization_barrier((all_query, next_sum))
    query_pieces = pieces(term(all_query))
    kv_grad = project_pair([near[:count], next_sum], cosine, -sine)
    all_kv_grad = reorder(key_meta, lax.all_gather(kv_grad, "row", axis=0, tiled=True))
    pair_term, query_pieces = lax.optimization_barrier((term(all_kv_grad), query_pieces))
    grad_query = total(query_pieces)
    grad_pair = total(pieces(pair_term))
    pair = w_key.shape[1]
    return context[None], grad_query, grad_pair[:, :pair], grad_pair[:, pair:]


def solution(mesh):
    in_specs = (
        P("depth", "row", "col"),
        P(("row", "depth"), "col"),
        P(("row", "depth"), "col"),
        P(("row", "depth"), "col"),
        P("depth", "row", "col"),
        P("depth", "row"),
        P(),
    )
    out_specs = (
        P("depth", "row", "col"),
        P(("row", "depth"), "col"),
        P(("row", "depth"), "col"),
        P(("row", "depth"), "col"),
    )
    return jax.shard_map(shards, mesh=mesh, in_specs=in_specs, out_specs=out_specs, check_vma=False)
```
